128 devices in a mesh: engine: 16 (over x, z), tp: 8 (over y, core).
Axes of the slice: x: 4, y: 4, z: 4, core: 2. Of those that a mesh axis runs over, the one named last changes fastest.
Arguments:
- kv_pool: bfloat16 [1792, 8, 128, 256], P('engine', 'tp'), may hold values from -6 to 6
- page_table: int32 [256, 7], P('engine'), may hold values from 0 to 111, as said below
- hist_len: int32 [256], replicated, may hold values from 1 to 895, as said below
- new_slot: int32 [256], replicated, may hold values from 0 to 255, as said below
- dec_q: bfloat16 [256, 8192], P('engine', 'tp'), may hold values from -6 to 6
- dec_kv: bfloat16 [256, 8, 256], P('engine', 'tp'), may hold values from -6 to 6
- tool_q: bfloat16 [8192, 8192], P('engine', 'tp'), may hold values from -6 to 6
- tool_kv: bfloat16 [8192, 8, 256], P('engine', 'tp'), may hold values from -6 to 6
- w_out: bfloat16 [8192, 8192], P('tp'), may hold values from -0.0625 to 0.0625
Outputs:
- dec_out: bfloat16 [256, 8192], P('engine', 'tp')
- tool_out: bfloat16 [8192, 8192], P('engine', 'tp')
The draws below stay inside these ranges and needn't reach their ends.
Inputs may be any that keep to these rules, and one draw needn't show every extreme that they name: `page_table`: entry [g, p] is a page of the pool of conversation g's engine, rows (g // 16) * 112 onward of kv_pool; the 16 conversations of one engine use each of its 112 pages exactly once. `hist_len`: the largest value is reached in every draw. A permutation; conversation g moves to engine new_slot[g] // 16. Every engine receives exactly 16 conversations; of the conversations of one old engine at most 2 go to the same new engine, and exactly 2 for some pair of engines in every draw.
All inputs are finite; a program needn't handle non-finite values.
Results may differ from the reference program's by a relative error of at most 0.02.
Values may be sent and summed in bfloat16 or wider, within the bound.
A program may use at most 128 MiB of HBM per device.

```python
import jax
import jax.numpy as jnp
from jax import lax

D = 8192
QH = 64
KVH = 8
HD = 128
PAGE = 128
PAGES_MAX = 7
CONV_DEV = 16
TOOL = 32
MAXLEN = 896
POOL = 112
CONVS = 256
POOL_ALL = 1792
TOOL_ROWS = 8192
GROUPS = 8


def draw_kv_pool(key, part):
    key = jax.random.fold_in(key, 21)
    key_one = jax.random.fold_in(key, 0)
    pool_shape = (POOL_ALL, KVH, PAGE, 2 * HD)
    values = jnp.clip(jax.random.normal(key_one, pool_shape, jnp.float32), -6.0, 6.0)
    return values.astype(jnp.bfloat16)


def draw_dec_q(key, part):
    key = jax.random.fold_in(key, 31)
    key_one = jax.random.fold_in(key, 0)
    values = jnp.clip(jax.random.normal(key_one, (CONVS, QH * HD), jnp.float32), -6.0, 6.0)
    return values.astype(jnp.bfloat16)


def draw_tool_q(key, part):
    key = jax.random.fold_in(key, 41)
    key_one = jax.random.fold_in(key, 0)
    values = jnp.clip(jax.random.normal(key_one, (TOOL_ROWS, QH * HD), jnp.float32), -6.0, 6.0)
    return values.astype(jnp.bfloat16)


def draw_page_table(key, part):
    key = jax.random.fold_in(key, 7)
    engines = CONVS // CONV_DEV
    perms = jax.vmap(lambda subkey: jax.random.permutation(subkey, POOL))(jax.random.split(key, engines))
    return perms.reshape(CONVS, PAGES_MAX).astype(jnp.int32)


def draw_hist_len(key, part):
    key = jax.random.fold_in(key, 5)
    key_one, key_two, key_three = jax.random.split(key, 3)
    engines = CONVS // CONV_DEV
    levels = 2 ** jax.random.randint(key_one, (engines,), 0, 4)
    spread = jnp.repeat(levels, CONV_DEV)
    base = jax.random.randint(key_two, (CONVS,), 0, MAXLEN - 1)
    lengths = MAXLEN - 1 - base * spread // 8
    longest = jax.random.randint(key_three, (), 0, CONVS)
    return jnp.where(jnp.arange(CONVS) == longest, MAXLEN - 1, lengths).astype(jnp.int32)


def draw_new_slot(key, part):
    key = jax.random.fold_in(key, 11)
    engines = CONVS // CONV_DEV
    doubled = max(CONV_DEV - engines, CONV_DEV // 4)
    single = CONV_DEV - 2 * doubled
    key_one, key_two, key_three, key_four = jax.random.split(key, 4)
    shifts = jax.random.permutation(key_one, engines)
    offsets = jnp.concatenate([shifts[:doubled], shifts[:doubled], shifts[doubled:doubled + single]])
    arrangement = jax.vmap(lambda subkey: jax.random.permutation(subkey, CONV_DEV))(jax.random.split(key_two, engines))
    relabel = jax.random.permutation(key_three, engines)
    engine_ids = jnp.arange(engines, dtype=jnp.int32)[:, None]
    target = relabel[(engine_ids + offsets[arrangement]) % engines].reshape(-1)
    all_ids = jnp.arange(CONVS, dtype=jnp.int32)
    rank_in = jnp.sum((target[None, :] == target[:, None]) & (all_ids[None, :] < all_ids[:, None]), axis=1)
    seat_perms = jax.vmap(lambda subkey: jax.random.permutation(subkey, CONV_DEV))(jax.random.split(key_four, engines))
    return (target * CONV_DEV + seat_perms[target, rank_in]).astype(jnp.int32)


def level_of(key, dims, cuts, smallest, high):
    gain = 1.0
    for axis_at, parts in cuts:
        draws = jax.random.uniform(jax.random.fold_in(jax.random.fold_in(key, 6), axis_at), (parts,), jnp.float32, smallest / len(cuts), high / len(cuts))
        gain = gain * jnp.repeat(jnp.exp(draws), dims[axis_at] // parts).reshape((-1,) + (1,) * (len(dims) - 1 - axis_at))
    return gain


def noise(stream_key, dims, scale, bound, cuts=(), kind=jnp.bfloat16):
    values = jax.random.normal(stream_key, dims, jnp.float32) * scale
    if len(cuts) > 0:
        values = level_of(stream_key, dims, cuts, -0.22, 0.18) * values
    return jnp.clip(values, min=-bound, max=bound).astype(kind)


def setup_inputs(seed: int = 0) -> dict:
    seeds = jax.random.split(jax.random.key(seed), 10)
    return {
        "kv_pool": draw_kv_pool(jax.random.fold_in(seeds[9], 71), 0),
        "page_table": draw_page_table(jax.random.fold_in(seeds[9], 71), 0),
        "hist_len": draw_hist_len(jax.random.fold_in(seeds[9], 71), 0),
        "new_slot": draw_new_slot(jax.random.fold_in(seeds[9], 71), 0),
        "dec_q": draw_dec_q(jax.random.fold_in(seeds[9], 71), 0),
        "dec_kv": noise(seeds[5], (CONVS, KVH, 2 * HD), 1.0, 6.0, ((0, 16), (1, 8))),
        "tool_q": draw_tool_q(jax.random.fold_in(seeds[9], 71), 0),
        "tool_kv": noise(seeds[7], (TOOL_ROWS, KVH, 2 * HD), 1.0, 6.0, ((0, 16), (1, 8))),
        "w_out": noise(seeds[8], (QH * HD, D), (QH * HD) ** -0.5, 0.0625, ((0, 8),)),
    }


def conversation_cache(kv_pool, page_table, hist_len, dec_kv, conv_id):
    engine_id = conv_id // CONV_DEV
    page_rows = kv_pool[engine_id * POOL + page_table[conv_id]]
    position = jnp.arange(MAXLEN, dtype=jnp.int32).reshape(PAGES_MAX, PAGE)
    written = position == hist_len[conv_id]
    page_rows = jnp.where(written[:, None, :, None], dec_kv[conv_id][None, :, None, :], page_rows)
    return jnp.transpose(page_rows, (0, 2, 1, 3)).reshape(MAXLEN, KVH, 2 * HD)


def attend(queries, key_rows, allowed):
    scores = jnp.einsum('rhgd,lhd->rhgl', queries.astype(jnp.float32), key_rows[..., :HD].astype(jnp.float32)) * (HD ** -0.5)
    scores = jnp.where(allowed[:, None, None, :], scores, -jnp.inf)
    row_peak = jnp.max(scores, axis=3, keepdims=True)
    exponent = jnp.exp(scores - row_peak)
    row_total = jnp.sum(exponent, axis=3)
    weights = exponent.astype(jnp.bfloat16)
    weighted = jnp.einsum('rhgl,lhd->rhgd', weights.astype(jnp.float32), key_rows[..., HD:].astype(jnp.float32))
    return (weighted / row_total[..., None]).astype(jnp.bfloat16).reshape(queries.shape[0], -1)


def project(attn, w_out):
    part_width = attn.shape[1] // GROUPS
    summed = jnp.zeros((attn.shape[0], w_out.shape[1]), jnp.float32)
    for group_index in range(GROUPS):
        lower = group_index * part_width
        partial_sum = jnp.dot(attn[:, lower:lower + part_width], w_out[lower:lower + part_width], preferred_element_type=jnp.float32)
        partial_sum = lax.optimization_barrier(partial_sum.astype(jnp.bfloat16))
        summed = summed + partial_sum.astype(jnp.float32)
    return summed.astype(jnp.bfloat16)


def reference(kv_pool, page_table, hist_len, new_slot, dec_q, dec_kv, tool_q, tool_kv, w_out):
    group_size = QH // KVH
    position = jnp.arange(MAXLEN, dtype=jnp.int32)

    def decode_one(conv_id):
        key_rows = conversation_cache(kv_pool, page_table, hist_len, dec_kv, conv_id)
        queries = dec_q[conv_id].reshape(1, KVH, group_size, HD)
        allowed = (position <= hist_len[conv_id])[None]
        return attend(queries, key_rows, allowed)[0]

    dec_attn = lax.map(decode_one, jnp.arange(CONVS, dtype=jnp.int32))
    anchor = jnp.argsort(new_slot).astype(jnp.int32)
    tool_order = jnp.arange(TOOL, dtype=jnp.int32)

    def prefill_one(new_index):
        conv_id = anchor[new_index]
        cached = conversation_cache(kv_pool, page_table, hist_len, dec_kv, conv_id)
        fresh_kv = lax.dynamic_slice_in_dim(tool_kv, (new_index * TOOL).astype(jnp.int32), TOOL)
        key_rows = jnp.concatenate([cached, fresh_kv], axis=0)
        queries = lax.dynamic_slice_in_dim(tool_q, (new_index * TOOL).astype(jnp.int32), TOOL).reshape(TOOL, KVH, group_size, HD)
        prefix_mask = jnp.broadcast_to((position <= hist_len[conv_id])[None], (TOOL, MAXLEN))
        causal_mask = tool_order[None, :] <= tool_order[:, None]
        allowed = jnp.concatenate([prefix_mask, causal_mask], axis=1)
        return attend(queries, key_rows, allowed)

    tool_attn = lax.map(prefill_one, jnp.arange(CONVS, dtype=jnp.int32)).reshape(TOOL_ROWS, QH * HD)
    return project(dec_attn, w_out), project(tool_attn, w_out)
```

```python
import functools
import math

import jax
import jax.numpy as jnp
from jax import lax
from jax.experimental import pallas as pl
from jax.experimental.pallas import tpu as pltpu
from jax.sharding import PartitionSpec as P

NEG = -1e30


def plan(page_table, hist_len, new_slot, engine_id, engines):
    conv_dev = page_table.shape[0]
    half = conv_dev // 2
    slot = new_slot.reshape(engines, conv_dev)
    target = slot // conv_dev
    ids = jnp.arange(conv_dev, dtype=jnp.int32)
    before = ids[None, :] < ids[:, None]
    same = target[:, :, None] == target[:, None, :]
    rank = jnp.sum(same & before, axis=2, dtype=jnp.int32)
    doubled = jnp.sum(same, axis=2, dtype=jnp.int32) > 1
    lone_before = jnp.sum(before[None] & ~doubled[:, None, :], axis=2, dtype=jnp.int32)
    pairs = jnp.sum(doubled, axis=1, dtype=jnp.int32)[:, None] // 2
    color = jnp.where(doubled, rank, (lone_before >= half - pairs).astype(jnp.int32))
    place = jnp.sum((color[:, :, None] == color[:, None, :]) & before, axis=2, dtype=jnp.int32)
    colors = jnp.arange(2, dtype=jnp.int32)
    peers = jnp.arange(engines, dtype=jnp.int32)
    out_mask = (target == engine_id)[None] & (color[None] == colors[:, None, None])
    send = jnp.sum(jnp.where(out_mask, (slot % conv_dev)[None], 0), axis=2, dtype=jnp.int32).reshape(-1)
    home = slot[None] == (engine_id * conv_dev + ids)[:, None, None]
    final = jnp.sum(jnp.where(home, (color * engines + peers[:, None])[None], 0), axis=(1, 2), dtype=jnp.int32)
    my_target = lax.dynamic_index_in_dim(target, engine_id, 0, False)
    my_color = lax.dynamic_index_in_dim(color, engine_id, 0, False)
    my_place = lax.dynamic_index_in_dim(place, engine_id, 0, False)
    my_hist = lax.dynamic_slice_in_dim(hist_len, engine_id * conv_dev, conv_dev)
    row = my_color * half + my_place
    at = row[None, :] == ids[:, None]
    pick = lambda v: jnp.sum(jnp.where(at, v[None], 0), axis=1, dtype=jnp.int32)
    conv = pick(ids)
    parcel = pick(my_color * engines + my_target)
    hist = pick(my_hist)
    pages = jnp.sum(jnp.where(at[:, :, None], page_table[None], 0), axis=1, dtype=jnp.int32)
    back_mask = (my_target[None] == peers[:, None])[None] & (my_color[None, None] == colors[:, None, None])
    back = jnp.sum(jnp.where(back_mask, row[None, None], 0), axis=2, dtype=jnp.int32).reshape(-1)
    return dict(send=send, final=final, conv=conv, parcel=parcel, hist=hist, pages=pages, back=back, row=row)


def attend(tool_q, tool_kv, dec_q, dec_kv, pages, hist, score_scale):
    tool, head = tool_q.shape[0], dec_q.shape[1]
    group = tool_q.shape[1] // head
    page = pages[0].shape[0]
    queries = jnp.concatenate([tool_q[:, h * head : (h + 1) * head] for h in range(group)] + [dec_q], axis=0)
    rows, prefix = queries.shape[0], len(pages) * page
    fresh = jnp.concatenate(
        [tool_kv, dec_kv, jnp.zeros((page - tool - 16, 2 * head), tool_kv.dtype)],
        axis=0,
    )
    kv = jnp.concatenate(list(pages) + [fresh], axis=0)
    scores = lax.dot_general(
        queries, kv[:, :head], (((1,), (1,)), ((), ())), preferred_element_type=jnp.float32
    )
    old = jnp.where(lax.broadcasted_iota(jnp.int32, (1, prefix), 1) < hist, 0.0, NEG)
    col = lax.broadcasted_iota(jnp.int32, (rows, page), 1)
    row = lax.broadcasted_iota(jnp.int32, (rows, page), 0)
    near = ((col <= row % tool) & (row < group * tool)) | (col == tool)
    scores = jnp.concatenate(
        [scores[:, :prefix] + old, jnp.where(near, scores[:, prefix:], NEG)], axis=1
    )
    peak = jnp.max(scores, axis=1, keepdims=True)
    weights = jnp.exp2((scores - peak) * (score_scale * math.log2(math.e)))
    total = jnp.sum(weights, axis=1, keepdims=True)
    mixed = jnp.dot(weights.astype(jnp.bfloat16), kv[:, head:], preferred_element_type=jnp.float32)
    return (mixed / total).astype(jnp.bfloat16)


def attention_kernel(scale, conv_s, parcel_s, hist_s, pages_s, pool, tool_q, tool_kv, dec_q, dec_kv, out, dec_out):
    k = pl.program_id(0)
    conv, parcel = conv_s[k], parcel_s[k]
    pages = [pool[pages_s[k, p]] for p in range(pages_s.shape[1])]
    got = attend(
        tool_q[parcel], tool_kv[parcel], dec_q[conv], dec_kv[conv], pages, hist_s[k], scale
    )
    tool, head = tool_q.shape[1], dec_q.shape[2]
    group = tool_q.shape[2] // head
    for h in range(group):
        out[0, :, h * head : (h + 1) * head] = got[h * tool : (h + 1) * tool]
    dec_out[0] = got[group * tool :]


def local(kv_pool, page_table, hist_len, new_slot, dec_q, dec_kv, tool_q, tool_kv, w_out):
    engines = lax.axis_size("engine")
    engine_id = lax.axis_index("engine")
    conv_dev, pages_max = page_table.shape
    page_len, head = kv_pool.shape[2], kv_pool.shape[3] // 2
    group = dec_q.shape[1] // head
    tool = tool_q.shape[0] // conv_dev
    width = group * head
    t = plan(page_table, hist_len, new_slot, engine_id, engines)
    both = jnp.concatenate([tool_q, tool_kv[:, 0]], axis=1).reshape(conv_dev, tool, -1)
    parcels = both[t["send"]].reshape(2, engines, tool, -1)
    came = lax.all_to_all(parcels, "engine", split_axis=1, concat_axis=1, tiled=True)
    came = came.reshape(2 * engines, tool, -1)
    dec16 = jnp.pad(dec_q.reshape(conv_dev, group, head), ((0, 0), (0, 16 - group), (0, 0)))
    whole = lambda shape: pl.BlockSpec(shape, lambda k, *_: (0,) * len(shape))
    got, dec_got = pl.pallas_call(
        functools.partial(attention_kernel, head**-0.5),
        grid_spec=pltpu.PrefetchScalarGridSpec(
            num_scalar_prefetch=4,
            grid=(conv_dev,),
            in_specs=[
                whole((kv_pool.shape[0], page_len, 2 * head)),
                whole((2 * engines, tool, width)),
                whole((2 * engines, tool, 2 * head)),
                whole((conv_dev, 16, head)),
                whole((conv_dev, 16, 2 * head)),
            ],
            out_specs=[
                pl.BlockSpec((1, tool, width), lambda k, *_: (k, 0, 0)),
                pl.BlockSpec((1, 16, head), lambda k, *_: (k, 0, 0)),
            ],
        ),
        out_shape=[
            jax.ShapeDtypeStruct((conv_dev, tool, width), jnp.bfloat16),
            jax.ShapeDtypeStruct((conv_dev, 16, head), jnp.bfloat16),
        ],
        compiler_params=pltpu.CompilerParams(vmem_limit_bytes=56 * 2**20),
    )(
        t["conv"], t["parcel"], t["hist"], t["pages"],
        kv_pool[:, 0], came[..., :width], came[..., width:], dec16, jnp.broadcast_to(dec_kv, (conv_dev, 16, 2 * head)),
    )
    attn = jnp.concatenate([got.reshape(conv_dev * tool, width), dec_got[:, :group].reshape(conv_dev, width)])
    sums = lax.psum_scatter(
        jnp.dot(attn, w_out, preferred_element_type=jnp.float32).astype(jnp.bfloat16),
        "tp", scatter_dimension=1, tiled=True,
    )
    rows = sums[: conv_dev * tool].reshape(conv_dev, tool, -1)
    dec_out = sums[conv_dev * tool :][t["row"]]
    back = rows[t["back"]].reshape(2, engines, tool, -1)
    home = lax.all_to_all(back, "engine", split_axis=1, concat_axis=1, tiled=True)
    tool_out = home.reshape(2 * engines, tool, -1)[t["final"]].reshape(conv_dev * tool, -1)
    return dec_out, tool_out


def solution(mesh):
    return jax.shard_map(
        local,
        mesh=mesh,
        in_specs=(
            P("engine", "tp", None, None),
            P("engine", None),
            P(),
            P(),
            P("engine", "tp"),
            P("engine", "tp", None),
            P("engine", "tp"),
            P("engine", "tp", None),
            P("tp", None),
        ),
        out_specs=(P("engine", "tp"), P("engine", "tp")),
        check_vma=False,
    )
```

```python
import functools
import math

import jax
import jax.numpy as jnp
from jax import lax
from jax.experimental import pallas as pl
from jax.experimental.pallas import tpu as pltpu
from jax.sharding import PartitionSpec as P

NEG = -1e30
MESH = pl.DeviceIdType.MESH
BF16, F32 = jnp.bfloat16, jnp.float32
COLORS = 2
CUTS = 2
CHIPS = 4


def plan(page_table, hist_len, new_slot, engine_id, engines):
    conv_dev = page_table.shape[0]
    half = conv_dev // 2
    slot = new_slot.reshape(engines, conv_dev)
    target = slot // conv_dev
    ids = jnp.arange(conv_dev, dtype=jnp.int32)
    before = ids[None, :] < ids[:, None]
    same = target[:, :, None] == target[:, None, :]
    rank = jnp.sum(same & before, axis=2, dtype=jnp.int32)
    doubled = jnp.sum(same, axis=2, dtype=jnp.int32) > 1
    lone_before = jnp.sum(before[None] & ~doubled[:, None, :], axis=2, dtype=jnp.int32)
    pairs = jnp.sum(doubled, axis=1, dtype=jnp.int32)[:, None] // 2
    color = jnp.where(doubled, rank, (lone_before >= half - pairs).astype(jnp.int32))
    place = jnp.sum((color[:, :, None] == color[:, None, :]) & before, axis=2, dtype=jnp.int32)
    colors = jnp.arange(2, dtype=jnp.int32)
    peers = jnp.arange(engines, dtype=jnp.int32)
    out_mask = (target == engine_id)[None] & (color[None] == colors[:, None, None])
    send = jnp.sum(jnp.where(out_mask, (slot % conv_dev)[None], 0), axis=2, dtype=jnp.int32).reshape(-1)
    home = slot[None] == (engine_id * conv_dev + ids)[:, None, None]
    final = jnp.sum(jnp.where(home, (color * engines + peers[:, None])[None], 0), axis=(1, 2), dtype=jnp.int32)
    my_target = lax.dynamic_index_in_dim(target, engine_id, 0, False)
    my_color = lax.dynamic_index_in_dim(color, engine_id, 0, False)
    my_place = lax.dynamic_index_in_dim(place, engine_id, 0, False)
    my_hist = lax.dynamic_slice_in_dim(hist_len, engine_id * conv_dev, conv_dev)
    row = my_color * half + my_place
    at = row[None, :] == ids[:, None]
    pick = lambda v: jnp.sum(jnp.where(at, v[None], 0), axis=1, dtype=jnp.int32)
    pages = jnp.sum(jnp.where(at[:, :, None], page_table[None], 0), axis=1, dtype=jnp.int32)
    back_mask = (my_target[None] == peers[:, None])[None] & (my_color[None, None] == colors[:, None, None])
    back = jnp.sum(jnp.where(back_mask, my_place[None, None], 0), axis=2, dtype=jnp.int32).reshape(-1)
    return jnp.concatenate(
        [send, back, final, pick(ids), pick(my_target), my_hist, pick(my_hist)]
        + [page_table.reshape(-1), pages.reshape(-1)]
    ).astype(jnp.int32)


def attend(queries, pages, fresh, bias, near, scale):
    head = queries.shape[1]
    kv = jnp.concatenate(list(pages) + [fresh], axis=0)
    prefix = bias.shape[1]
    scores = lax.dot_general(queries, kv[:, :head], (((1,), (1,)), ((), ())), preferred_element_type=F32)
    near = jnp.concatenate([near] * (queries.shape[0] // near.shape[0]), axis=0)
    scores = jnp.concatenate([scores[:, :prefix] + bias, scores[:, prefix:] + near], axis=1)
    peak = jnp.max(scores, axis=1, keepdims=True)
    weights = jnp.exp2((scores - peak) * (scale * math.log2(math.e)))
    total = jnp.sum(weights, axis=1, keepdims=True)
    mixed = jnp.dot(weights.astype(BF16), kv[:, head:], preferred_element_type=F32)
    return mixed / total


def kernel(
    tab, pool_hbm, w_hbm, tool_q, tool_kv, dec_q, dec_kv, out, dec_out,
    pool, w, fsend, frecv_0, frecv_1, frecv_2, frecv_3, attn0, attn, heads, part0, part, got0, got, sums0, sums,
    two0, two, direct0, direct, rows0, rows, bsend, brecv,
    pool_sem, w_sem, fs, fr, xs, xr, ys, yr, bs, br,
    *, engines, conv_dev, pages_max,
):
    stages = COLORS * CUTS
    frecv = [frecv_0, frecv_1, frecv_2, frecv_3]
    half = conv_dev // COLORS
    cut = tool_q.shape[2]
    head = dec_q.shape[2]
    width = tool_q.shape[3]
    group = width // head
    page = pool.shape[1]
    prefix = pages_max * page
    scale = head**-0.5
    width_out = w.shape[2]
    side = width_out // 2
    main = half * cut
    SEND, BACK = 0, COLORS * engines
    FINAL = BACK + COLORS * engines
    CONV = FINAL + conv_dev
    DEST = CONV + conv_dev
    HIST = DEST + conv_dev
    PAGES = HIST + 2 * conv_dev

    me, tp = lax.axis_index("engine"), lax.axis_index("tp")
    y, core = tp // 2, tp % 2
    partner = (me, y * 2 + 1 - core)
    up = (me, (y + 1) % CHIPS * 2 + core)
    down = (me, (y + CHIPS - 1) % CHIPS * 2 + core)
    other = lambda k: lax.rem(me + k, engines)

    barrier = pltpu.get_barrier_semaphore()

    @pl.loop(1, engines)
    def _(k):
        pl.semaphore_signal(barrier, inc=1, device_id=(other(k), tp), device_id_type=MESH)

    for peer in (partner, up, down):
        pl.semaphore_signal(barrier, inc=1, device_id=peer, device_id_type=MESH)

    load_pool = pltpu.make_async_copy(pool_hbm, pool, pool_sem)
    load_pool.start()
    load_w = [
        pltpu.make_async_copy(w_hbm.at[:, pl.ds(b * width_out, width_out)], w.at[b], w_sem.at[b])
        for b in range(2 * CHIPS)
    ]

    def fill(ref, s, engine):
        slot = tab[SEND + s // CUTS * engines + engine]
        ref[engine, :, :width] = tool_q[slot, s % CUTS]
        ref[engine, :, width:] = tool_kv[slot, s % CUTS]

    def fwd(s, k):
        return pltpu.make_async_remote_copy(
            fsend.at[s, other(k)], frecv[s].at[me], fs.at[s, other(k)], fr.at[s, me],
            device_id=(other(k), tp), device_id_type=MESH,
        )

    def fwd_in(s, k):
        return pltpu.make_async_remote_copy(
            fsend.at[s, me], frecv[s].at[other(k)], fs.at[s, me], fr.at[s, other(k)],
            device_id=(other(k), tp), device_id_type=MESH,
        )

    for s in range(stages):

        @pl.loop(1, engines)
        def _(k, s=s):
            fill(fsend.at[s], s, other(k))

        if s == 0:
            pl.semaphore_wait(barrier, engines - 1 + 3)

        @pl.loop(1, engines)
        def _(k, s=s):
            fwd(s, k).start()

        fill(frecv[s], s, me)
    for copy in load_w:
        copy.start()

    def pages_of(row):
        return [pool[tab[PAGES + row * pages_max + p]] for p in range(pages_max)]

    def bias_of(row):
        return jnp.where(lax.broadcasted_iota(jnp.int32, (1, prefix), 1) < tab[HIST + row], 0.0, NEG)

    col = lax.broadcasted_iota(jnp.int32, (16, page), 1)
    row = lax.broadcasted_iota(jnp.int32, (16, page), 0)

    load_pool.wait()
    only = jnp.where(col == 0, 0.0, NEG)

    @pl.loop(0, conv_dev)
    def _(i):
        fresh = jnp.concatenate([dec_kv[i], jnp.zeros((page - 16, 2 * head), BF16)], axis=0)
        got_i = attend(dec_q[i], pages_of(i), fresh, bias_of(i), only, scale)
        for h in range(group):
            heads[h, pl.ds(i, 1), :] = got_i[h : h + 1]

    for h in range(group):
        attn0[main:, h * head : (h + 1) * head] = heads[h].astype(BF16)

    def of(first, later, s):
        return first if s == 0 else later.at[s - 1]

    def attention(s):
        color, u = s // CUTS, s % CUTS

        @pl.loop(1, engines)
        def _(k):
            fwd_in(s, k).wait_recv()

        known = (u + 1) * cut
        near = jnp.where(((col <= row + u * cut) & (col < known)) | (col == known), 0.0, NEG)
        dst = of(attn0, attn, s)

        @pl.loop(0, half)
        def _(j):
            conv = tab[CONV + color * half + j]
            at = conv_dev + color * half + j
            dest = tab[DEST + color * half + j]
            kv_new = [frecv[color * CUTS + v][dest, :, width:] for v in range(u + 1)]
            fresh = jnp.concatenate(
                kv_new + [dec_kv[conv], jnp.zeros((page - 16 - known, 2 * head), BF16)], axis=0
            )
            q = frecv[s][dest, :, :width]
            queries = jnp.concatenate([q[:, h * head : (h + 1) * head] for h in range(group)], axis=0)
            got_j = attend(queries, pages_of(at), fresh, bias_of(at), near, scale).astype(BF16)
            for h in range(group):
                dst[pl.ds(pl.multiple_of(j * cut, cut), cut), h * head : (h + 1) * head] = got_j[
                    h * cut : (h + 1) * cut
                ]

    def swap(s, k):
        return pltpu.make_async_remote_copy(
            of(part0, part, s).at[2 * k], of(got0, got, s).at[k], xs.at[s, k], xr.at[s, k],
            device_id=partner, device_id_type=MESH,
        )

    def hop(s, n, src, dst, to):
        return pltpu.make_async_remote_copy(src, dst, ys.at[s, n], yr.at[s, n], device_id=to, device_id_type=MESH)

    def ring(s):
        a, t, d = of(sums0, sums, s), of(two0, two, s), of(direct0, direct, s)
        return [
            hop(s, 0, a.at[0, 0], t.at[0], up),
            hop(s, 1, a.at[0, 1], t.at[1], down),
            hop(s, 2, a.at[1, 1], d.at[0, 1], up),
            hop(s, 3, a.at[2, 0], d.at[1, 0], down),
            hop(s, 4, a.at[1, 0], d.at[0, 0], up),
            hop(s, 5, a.at[2, 1], d.at[1, 1], down),
        ]

    def finish(s, k):
        swap(s, k).wait_recv()
        mine, came, a = of(part0, part, s), of(got0, got, s), of(sums0, sums, s)
        for v in range(2):
            cols = slice(v * side, (v + 1) * side)
            a[k, v] = (mine[2 * k + 1, :, cols].astype(F32) + came[k, :, cols].astype(F32)).astype(BF16)

    def project(s):
        src, dst = of(attn0, attn, s), of(part0, part, s)
        steps = ring(s)

        @pl.loop(0, 2 * CHIPS)
        def _(b):
            k = b // 2
            far = lax.rem(2 - k - k // 2 + 2 * (k // 3) + y + CHIPS, CHIPS)
            block = far * 2 + lax.rem(core + 1 + b % 2, 2)
            dst[b] = jnp.dot(src[...], w[block], preferred_element_type=F32).astype(BF16)

            @pl.when(b % 2 == 0)
            def _():
                swap(s, k).start()

            @pl.when((b % 2 == 1) & (b > 1))
            def _():
                finish(s, k - 1)

            @pl.when(b == 3)
            def _():
                steps[0].start()
                steps[1].start()

            @pl.when(b == 5)
            def _():
                steps[2].start()

            @pl.when(b == 7)
            def _():
                steps[3].start()

        finish(s, CHIPS - 1)

    def relay(s):
        a, t, steps = of(sums0, sums, s), of(two0, two, s), ring(s)
        for v, k in ((0, 1), (1, 2)):
            steps[v].wait_recv()
            a[k, v] = (a[k, v].astype(F32) + t[v].astype(F32)).astype(BF16)
            steps[4 + v].start()

    def back(s, k):
        color, u = s // CUTS, s % CUTS
        return pltpu.make_async_remote_copy(
            bsend.at[s, other(k)], brecv.at[u, color * engines + me], bs.at[s, other(k)], br.at[s, me],
            device_id=(other(k), tp), device_id_type=MESH,
        )

    def back_in(s, k):
        color, u = s // CUTS, s % CUTS
        return pltpu.make_async_remote_copy(
            bsend.at[s, me], brecv.at[u, color * engines + other(k)], bs.at[s, me], br.at[s, other(k)],
            device_id=(other(k), tp), device_id_type=MESH,
        )

    def deliver(s):
        color, u = s // CUTS, s % CUTS
        a, d, dst = of(sums0, sums, s), of(direct0, direct, s), of(rows0, rows, s)
        steps = ring(s)
        for n in range(2, 6):
            steps[n].wait_recv()
        for v in range(2):
            total = (a[3, v].astype(F32) + d[0, v].astype(F32) + d[1, v].astype(F32)).astype(BF16)
            dst[:, :, v * side : (v + 1) * side] = total.reshape(-1, cut, side)

        def mine(engine):
            place = tab[BACK + color * engines + engine]
            return dst[place]

        @pl.loop(1, engines)
        def _(k):
            bsend[s, other(k)] = mine(other(k))
            back(s, k).start()

        brecv[u, color * engines + me] = mine(me)
        if s == 0:
            dec_out[...] = dst[half]

    for s in range(stages):
        attention(s)
        if s == 0:
            for copy in load_w:
                copy.wait()
        else:
            relay(s - 1)
        project(s)
        if s > 0:
            deliver(s - 1)
    relay(stages - 1)
    deliver(stages - 1)

    for s in range(stages):

        @pl.loop(1, engines)
        def _(k, s=s):
            back_in(s, k).wait_recv()

    @pl.loop(0, conv_dev)
    def _(n):
        for u in range(CUTS):
            out[n, u] = brecv[u, tab[FINAL + n]]

    for s in range(stages):

        @pl.loop(1, engines)
        def _(k, s=s):
            fwd(s, k).wait_send()
            back(s, k).wait_send()

        for k in range(CHIPS):
            swap(s, k).wait_send()
        for step in ring(s):
            step.wait_send()


def local(kv_pool, page_table, hist_len, new_slot, dec_q, dec_kv, tool_q, tool_kv, w_out):
    engines = lax.axis_size("engine")
    conv_dev, pages_max = page_table.shape
    page, head = kv_pool.shape[2], kv_pool.shape[3] // 2
    width = dec_q.shape[1]
    group = width // head
    tool_rows = tool_q.shape[0]
    cut = tool_rows // conv_dev // CUTS
    width_out = w_out.shape[1] // (2 * CHIPS)
    side = width_out // 2
    stages = COLORS * CUTS
    main = conv_dev // COLORS * cut
    tab = plan(page_table, hist_len, new_slot, lax.axis_index("engine"), engines)
    dec16 = jnp.pad(dec_q.reshape(conv_dev, group, head), ((0, 0), (0, 16 - group), (0, 0)))
    kv16 = jnp.broadcast_to(dec_kv, (conv_dev, 16, 2 * head))
    vmem = lambda shape: pltpu.VMEM(shape, BF16)
    split = lambda lead, cols: [
        vmem(lead + (main + conv_dev, cols)),
        vmem((stages - 1,) + lead + (main, cols)),
    ]
    dma = pltpu.SemaphoreType.DMA
    in_vmem = pl.BlockSpec(memory_space=pltpu.VMEM)
    anywhere = pl.BlockSpec(memory_space=pl.ANY)
    tool_out, dec_out = pl.pallas_call(
        functools.partial(kernel, engines=engines, conv_dev=conv_dev, pages_max=pages_max),
        out_shape=[
            jax.ShapeDtypeStruct((conv_dev, CUTS, cut, width_out), BF16),
            jax.ShapeDtypeStruct((conv_dev, width_out), BF16),
        ],
        in_specs=[pl.BlockSpec(memory_space=pltpu.SMEM), anywhere, anywhere] + [in_vmem] * 4,
        out_specs=[in_vmem, in_vmem],
        scratch_shapes=[
            vmem((kv_pool.shape[0], page, 2 * head)),
            vmem((2 * CHIPS, w_out.shape[0], width_out)),
            vmem((stages, engines, cut, width + 2 * head)),
            *[vmem((engines, cut, width + 2 * head)) for _ in range(stages)],
            *split((), width),
            pltpu.VMEM((group, conv_dev, head), F32),
            *split((2 * CHIPS,), width_out),
            *split((CHIPS,), width_out),
            *split((CHIPS, 2), side),
            *split((2,), side),
            *split((2, 2), side),
            vmem((conv_dev // COLORS + 1, cut, width_out)),
            vmem((stages - 1, conv_dev // COLORS, cut, width_out)),
            vmem((stages, engines, cut, width_out)),
            vmem((CUTS, COLORS * engines, cut, width_out)),
            dma(()),
            dma((2 * CHIPS,)),
            dma((stages, engines)),
            dma((stages, engines)),
            dma((stages, CHIPS)),
            dma((stages, CHIPS)),
            dma((stages, 6)),
            dma((stages, 6)),
            dma((stages, engines)),
            dma((stages, engines)),
        ],
        compiler_params=pltpu.CompilerParams(
            collective_id=0, has_side_effects=True, vmem_limit_bytes=62 * 2**20
        ),
        cost_estimate=pl.CostEstimate(
            flops=2 * (tool_rows + conv_dev) * w_out.size, bytes_accessed=2 * (w_out.size + kv_pool.size), transcendentals=0
        ),
    )(
        tab, kv_pool[:, 0], w_out, tool_q.reshape(conv_dev, CUTS, cut, width),
        tool_kv.reshape(conv_dev, CUTS, cut, 2 * head), dec16, kv16,
    )
    return dec_out, tool_out.reshape(tool_rows, width_out)


def solution(mesh):
    return jax.shard_map(
        local,
        mesh=mesh,
        in_specs=(
            P("engine", "tp", None, None),
            P("engine", None),
            P(),
            P(),
            P("engine", "tp"),
            P("engine", "tp", None),
            P("engine", "tp"),
            P("engine", "tp", None),
            P("tp", None),
        ),
        out_specs=(P("engine", "tp"), P("engine", "tp")),
        check_vma=False,
    )
```

```python
import functools
import math

import jax
import jax.numpy as jnp
from jax import lax
from jax.experimental import pallas as pl
from jax.experimental.pallas import tpu as pltpu
from jax.sharding import PartitionSpec as P

NEG = -1e30
MESH = pl.DeviceIdType.MESH
BF16, F32 = jnp.bfloat16, jnp.float32
MAXIMUM = 2**30
COLORS = 2
CUTS = 2
TOGETHER = 2
FINAL, CONV, DEST, HIST, HIST_NAT, BACK, PAGES, PAGES_NAT = 0, 1, 2, 3, 4, 5, 8, 16
CHIPS = 4


def plan(slot, hist, pages, me, engines, conv_dev, table):
    half = conv_dev // COLORS
    i32 = jnp.int32
    lane = lax.broadcasted_iota(i32, slot.shape, 1)
    local_id = lane % conv_dev
    engine = lax.broadcasted_iota(i32, slot.shape, 0) * (128 // conv_dev) + lane // conv_dev
    target, seat = slot // conv_dev, slot % conv_dev
    zero = jnp.zeros(slot.shape, i32)

    def earlier(v, d):
        return pltpu.roll(v, d, 1), local_id >= d

    def later(v, d):
        return pltpu.roll(v, 128 - d, 1), local_id < conv_dev - d

    rank, twins = zero, zero
    for d in range(1, conv_dev):
        v, ok = earlier(target, d)
        rank = rank + jnp.where(ok & (v == target), 1, 0)
        v, ok = later(target, d)
        twins = twins + jnp.where(ok & (v == target), 1, 0)
    doubled = jnp.where(rank + twins > 0, 1, 0)
    ahead, behind = zero, zero
    for d in range(1, conv_dev):
        v, ok = earlier(doubled, d)
        ahead = ahead + jnp.where(ok, v, 0)
        v, ok = later(doubled, d)
        behind = behind + jnp.where(ok, v, 0)
    pairs = (ahead + doubled + behind) // 2
    color = jnp.where(doubled > 0, rank, jnp.where(local_id - ahead >= half - pairs, 1, 0))
    place = zero
    for d in range(1, conv_dev):
        v, ok = earlier(color, d)
        place = place + jnp.where(ok & (v == color), 1, 0)
    rows = slot.shape[0]
    for c in range(COLORS):
        v = jnp.where((target == me) & (color == c), seat, 0)
        d = 1
        while d < conv_dev:
            v = v + pltpu.roll(v, 128 - d, 1)
            d *= 2
        table[16 + c * rows : 16 + (c + 1) * rows, :] = jnp.minimum(v, conv_dev - 1)
    sub = lax.broadcasted_iota(i32, (conv_dev, 128), 0)

    def gather(match, value):
        total = jnp.zeros((conv_dev, 128), i32)
        for r in range(rows):
            hit = jnp.broadcast_to(match[r : r + 1], sub.shape) == sub
            total = total + jnp.where(hit, jnp.broadcast_to(value[r : r + 1], sub.shape), 0)
        return jnp.sum(total, axis=1, keepdims=True)

    mine = engine == me
    row = jnp.where(mine, color * half + place, -1)
    conv = gather(row, local_id)
    columns = [
        gather(jnp.where(target == me, seat, -1), color * engines + engine),
        conv,
        gather(row, target),
        gather(row, hist),
        gather(jnp.where(mine, local_id, -1), hist),
    ] + [gather(jnp.where(mine & (color == c), target, -1), place) for c in range(COLORS)]
    wide = lax.broadcasted_iota(i32, (conv_dev, 128), 1)
    result = jnp.zeros((conv_dev, 128), i32)
    most = [COLORS * engines - 1, conv_dev - 1, engines - 1, MAXIMUM, MAXIMUM] + [half - 1] * COLORS
    for c, (v, top) in enumerate(zip(columns, most)):
        result = jnp.where(wide == c, jnp.clip(v, 0, top), result)
    for p in range(pages.shape[0]):
        line = jnp.broadcast_to(jnp.concatenate([pages[p : p + 1], jnp.zeros((1, 128 - conv_dev), i32)], axis=1), sub.shape)
        by_row = jnp.sum(jnp.where(wide == conv, line, 0), axis=1, keepdims=True)
        by_conv = jnp.sum(jnp.where(wide == sub, line, 0), axis=1, keepdims=True)
        result = jnp.where(wide == PAGES + p, by_row, jnp.where(wide == PAGES_NAT + p, by_conv, result))
    table[:16, :] = result


def attend(queries, pages, fresh, bias, near, scale):
    head = queries.shape[1]
    kv = jnp.concatenate(list(pages) + [fresh], axis=0)
    prefix = bias.shape[1]
    scores = lax.dot_general(queries, kv[:, :head], (((1,), (1,)), ((), ())), preferred_element_type=F32)
    near = jnp.concatenate([near] * (queries.shape[0] // near.shape[0]), axis=0)
    scores = jnp.concatenate([scores[:, :prefix] + bias, scores[:, prefix:] + near], axis=1)
    peak = jnp.max(scores, axis=1, keepdims=True)
    weights = jnp.exp2((scores - peak) * (scale * math.log2(math.e)))
    total = jnp.sum(weights, axis=1, keepdims=True)
    mixed = jnp.dot(weights.astype(BF16), kv[:, head:], preferred_element_type=F32)
    return mixed / total


def kernel(
    new_slot, hist_len, page_table, pool_hbm, w_hbm, tool_q, tool_kv, dec_q, dec_kv, out, dec_out,
    table, tab, kv16, pool, w, fsend, frecv_0, frecv_1, frecv_2, frecv_3, attn0, attn, heads, part0, part, got0, got, sums0, sums,
    two0, two, direct0, direct, rows0, rows, bsend, brecv,
    tab_sem, pool_sem, w_sem, fs, fr, xs, xr, ys, yr, bs, br,
    *, engines, conv_dev, pages_max,
):
    stages = COLORS * CUTS
    frecv = [frecv_0, frecv_1, frecv_2, frecv_3]
    half = conv_dev // COLORS
    cut = tool_q.shape[2]
    head = pool.shape[2] // 2
    width = tool_q.shape[3]
    group = width // head
    page = pool.shape[1]
    prefix = pages_max * page
    scale = head**-0.5
    width_out = w.shape[2]
    side = width_out // 2
    main = half * cut
    me, tp = lax.axis_index("engine"), lax.axis_index("tp")
    y, core = tp // 2, tp % 2
    partner = (me, y * 2 + 1 - core)
    up = (me, (y + 1) % CHIPS * 2 + core)
    down = (me, (y + CHIPS - 1) % CHIPS * 2 + core)
    other = lambda k: lax.rem(me + k, engines)

    barrier = pltpu.get_barrier_semaphore()

    @pl.loop(1, engines)
    def _(k):
        pl.semaphore_signal(barrier, inc=1, device_id=(other(k), tp), device_id_type=MESH)

    for peer in (partner, up, down):
        pl.semaphore_signal(barrier, inc=1, device_id=peer, device_id_type=MESH)

    load_pool = pltpu.make_async_copy(pool_hbm, pool, pool_sem)
    load_pool.start()
    load_w = [
        pltpu.make_async_copy(w_hbm.at[:, pl.ds(b * width_out, width_out)], w.at[b], w_sem.at[b])
        for b in range(2 * CHIPS)
    ]
    plan(new_slot[...], hist_len[...], page_table[...], me, engines, conv_dev, table)
    load_tab = pltpu.make_async_copy(table, tab, tab_sem)
    load_tab.start()
    for h in range(group):
        heads[h] = dec_q[:, h * head : (h + 1) * head].astype(F32)
    dec_rows = dec_kv[...].astype(F32)
    for i in range(conv_dev):
        kv16[i] = jnp.broadcast_to(dec_rows[i : i + 1], (16, 2 * head)).astype(BF16)
    load_tab.wait()
    per_row = 128 // conv_dev

    def fill(ref, s, engine):
        slot = tab[16 + s // CUTS * (engines // per_row) + engine // per_row, engine % per_row * conv_dev]
        ref[engine, :, :width] = tool_q[slot, s % CUTS]
        ref[engine, :, width:] = tool_kv[slot, s % CUTS]

    def fwd(s, k):
        return pltpu.make_async_remote_copy(
            fsend.at[s, other(k)], frecv[s].at[me], fs.at[s, other(k)], fr.at[s, me],
            device_id=(other(k), tp), device_id_type=MESH,
        )

    def fwd_in(s, k):
        return pltpu.make_async_remote_copy(
            fsend.at[s, me], frecv[s].at[other(k)], fs.at[s, me], fr.at[s, other(k)],
            device_id=(other(k), tp), device_id_type=MESH,
        )

    for s in range(stages):

        @pl.loop(1, engines)
        def _(k, s=s):
            fill(fsend.at[s], s, other(k))

        if s == 0:
            pl.semaphore_wait(barrier, engines - 1 + 3)

        @pl.loop(1, engines)
        def _(k, s=s):
            fwd(s, k).start()

        fill(frecv[s], s, me)
    for copy in load_w:
        copy.start()

    def pages_of(row, first):
        return [pool[tab[row, first + p]] for p in range(pages_max)]

    def bias_of(row, column):
        return jnp.where(lax.broadcasted_iota(jnp.int32, (1, prefix), 1) < tab[row, column], 0.0, NEG)

    col = lax.broadcasted_iota(jnp.int32, (16, page), 1)
    row = lax.broadcasted_iota(jnp.int32, (16, page), 0)

    load_pool.wait()
    only = jnp.where(col == 0, 0.0, NEG)

    @pl.loop(0, conv_dev)
    def _(i):
        fresh = jnp.concatenate([kv16[i], jnp.zeros((page - 16, 2 * head), BF16)], axis=0)
        q = jnp.concatenate([heads[h, pl.ds(i, 1), :] for h in range(group)] + [jnp.zeros((16 - group, head), F32)], axis=0)
        got_i = attend(q.astype(BF16), pages_of(i, PAGES_NAT), fresh, bias_of(i, HIST_NAT), only, scale)
        for h in range(group):
            heads[h, pl.ds(i, 1), :] = got_i[h : h + 1]

    for h in range(group):
        attn0[main:, h * head : (h + 1) * head] = heads[h].astype(BF16)

    def of(first, later, s):
        return first if s == 0 else later.at[s - 1]

    def attention(s, between):
        color, u = s // CUTS, s % CUTS

        @pl.loop(1, engines)
        def _(k):
            fwd_in(s, k).wait_recv()

        known = (u + 1) * cut
        near = jnp.where(((col <= row + u * cut) & (col < known)) | (col == known), 0.0, NEG)
        dst = of(attn0, attn, s)

        def one(j):
            at = color * half + j
            conv, dest = tab[at, CONV], tab[at, DEST]
            kv_new = [frecv[color * CUTS + v][dest, :, width:] for v in range(u + 1)]
            fresh = jnp.concatenate(
                kv_new + [kv16[conv], jnp.zeros((page - 16 - known, 2 * head), BF16)], axis=0
            )
            q = frecv[s][dest, :, :width]
            queries = jnp.concatenate([q[:, h * head : (h + 1) * head] for h in range(group)], axis=0)
            return attend(queries, pages_of(at, PAGES), fresh, bias_of(at, HIST), near, scale).astype(BF16)

        def some(first, count):
            @pl.loop(0, count // TOGETHER)
            def _(i):
                js = [first + i * TOGETHER + n for n in range(TOGETHER)]
                for j, got_j in [(j, one(j)) for j in js]:
                    for h in range(group):
                        dst[pl.ds(pl.multiple_of(j * cut, cut), cut), h * head : (h + 1) * head] = got_j[
                            h * cut : (h + 1) * cut
                        ]

        some(0, half // 2)
        between()
        some(half // 2, half // 2)

    def swap(s, k):
        return pltpu.make_async_remote_copy(
            of(part0, part, s).at[2 * k], of(got0, got, s).at[k], xs.at[s, k], xr.at[s, k],
            device_id=partner, device_id_type=MESH,
        )

    def hop(s, n, src, dst, to):
        return pltpu.make_async_remote_copy(src, dst, ys.at[s, n], yr.at[s, n], device_id=to, device_id_type=MESH)

    def ring(s):
        a, t, d = of(sums0, sums, s), of(two0, two, s), of(direct0, direct, s)
        return [
            hop(s, 0, a.at[0, 0], t.at[0], up),
            hop(s, 1, a.at[0, 1], t.at[1], down),
            hop(s, 2, a.at[1, 1], d.at[0, 1], up),
            hop(s, 3, a.at[2, 0], d.at[1, 0], down),
            hop(s, 4, a.at[1, 0], d.at[0, 0], up),
            hop(s, 5, a.at[2, 1], d.at[1, 1], down),
        ]

    def finish(s, k):
        swap(s, k).wait_recv()
        mine, came, a = of(part0, part, s), of(got0, got, s), of(sums0, sums, s)
        for v in range(2):
            cols = slice(v * side, (v + 1) * side)
            a[k, v] = mine[2 * k + 1, :, cols] + came[k, :, cols]

    def project(s):
        src, dst = of(attn0, attn, s), of(part0, part, s)
        steps = ring(s)

        @pl.loop(0, 2 * CHIPS)
        def _(b):
            k = b // 2
            far = lax.rem(2 - k - k // 2 + 2 * (k // 3) + y + CHIPS, CHIPS)
            block = far * 2 + lax.rem(core + 1 + b % 2, 2)
            dst[b] = jnp.dot(src[...], w[block], preferred_element_type=F32).astype(BF16)

            @pl.when(b % 2 == 0)
            def _():
                swap(s, k).start()

            @pl.when((b % 2 == 1) & (b > 1))
            def _():
                finish(s, k - 1)

            @pl.when(b == 3)
            def _():
                steps[0].start()
                steps[1].start()

            @pl.when(b == 5)
            def _():
                steps[2].start()

            @pl.when(b == 7)
            def _():
                steps[3].start()

        finish(s, CHIPS - 1)

    def relay(s):
        a, t, steps = of(sums0, sums, s), of(two0, two, s), ring(s)
        for v, k in ((0, 1), (1, 2)):
            steps[v].wait_recv()
            a[k, v] = a[k, v] + t[v]
            steps[4 + v].start()

    def back(s, k):
        color, u = s // CUTS, s % CUTS
        return pltpu.make_async_remote_copy(
            bsend.at[s, other(k)], brecv.at[u, color * engines + me], bs.at[s, other(k)], br.at[s, me],
            device_id=(other(k), tp), device_id_type=MESH,
        )

    def back_in(s, k):
        color, u = s // CUTS, s % CUTS
        return pltpu.make_async_remote_copy(
            bsend.at[s, me], brecv.at[u, color * engines + other(k)], bs.at[s, me], br.at[s, other(k)],
            device_id=(other(k), tp), device_id_type=MESH,
        )

    def deliver(s):
        color, u = s // CUTS, s % CUTS
        a, d, dst = of(sums0, sums, s), of(direct0, direct, s), of(rows0, rows, s)
        steps = ring(s)
        for n in range(2, 6):
            steps[n].wait_recv()
        for v in range(2):
            total = (a[3, v].astype(F32) + d[0, v].astype(F32) + d[1, v].astype(F32)).astype(BF16)
            dst[:, :, v * side : (v + 1) * side] = total.reshape(-1, cut, side)

        def mine(engine):
            place = tab[engine, BACK + color]
            return dst[place]

        @pl.loop(1, engines)
        def _(k):
            bsend[s, other(k)] = mine(other(k))
            back(s, k).start()

        brecv[u, color * engines + me] = mine(me)
        if s == 0:
            dec_out[...] = dst[half]

    for s in range(stages):
        attention(s, (lambda s=s: relay(s - 1)) if s > 0 else (lambda: None))
        if s == 0:
            for copy in load_w:
                copy.wait()
        project(s)
        if s > 0:
            deliver(s - 1)
    relay(stages - 1)
    deliver(stages - 1)

    for s in range(stages):

        @pl.loop(1, engines)
        def _(k, s=s):
            back_in(s, k).wait_recv()

    @pl.loop(0, conv_dev)
    def _(n):
        for u in range(CUTS):
            out[n, u] = brecv[u, tab[n, FINAL]]

    for s in range(stages):

        @pl.loop(1, engines)
        def _(k, s=s):
            fwd(s, k).wait_send()
            back(s, k).wait_send()

        for k in range(CHIPS):
            swap(s, k).wait_send()
        for step in ring(s):
            step.wait_send()


def local(kv_pool, page_table, hist_len, new_slot, dec_q, dec_kv, tool_q, tool_kv, w_out):
    engines = lax.axis_size("engine")
    conv_dev, pages_max = page_table.shape
    page, head = kv_pool.shape[2], kv_pool.shape[3] // 2
    width = dec_q.shape[1]
    group = width // head
    tool_rows = tool_q.shape[0]
    cut = tool_rows // conv_dev // CUTS
    width_out = w_out.shape[1] // (2 * CHIPS)
    side = width_out // 2
    stages = COLORS * CUTS
    main = conv_dev // COLORS * cut
    vmem = lambda shape: pltpu.VMEM(shape, BF16)
    split = lambda lead, cols: [
        vmem(lead + (main + conv_dev, cols)),
        vmem((stages - 1,) + lead + (main, cols)),
    ]
    dma = pltpu.SemaphoreType.DMA
    in_vmem = pl.BlockSpec(memory_space=pltpu.VMEM)
    anywhere = pl.BlockSpec(memory_space=pl.ANY)
    tool_out, dec_out = pl.pallas_call(
        functools.partial(kernel, engines=engines, conv_dev=conv_dev, pages_max=pages_max),
        out_shape=[
            jax.ShapeDtypeStruct((conv_dev, CUTS, cut, width_out), BF16),
            jax.ShapeDtypeStruct((conv_dev, width_out), BF16),
        ],
        in_specs=[in_vmem] * 3 + [anywhere] * 2 + [in_vmem] * 4,
        out_specs=[in_vmem, in_vmem],
        scratch_shapes=[
            pltpu.VMEM((24, 128), jnp.int32),
            pltpu.SMEM((24, 128), jnp.int32),
            vmem((conv_dev, 16, 2 * head)),
            vmem((kv_pool.shape[0], page, 2 * head)),
            vmem((2 * CHIPS, w_out.shape[0], width_out)),
            vmem((stages, engines, cut, width + 2 * head)),
            *[vmem((engines, cut, width + 2 * head)) for _ in range(stages)],
            *split((), width),
            pltpu.VMEM((group, conv_dev, head), F32),
            *split((2 * CHIPS,), width_out),
            *split((CHIPS,), width_out),
            *split((CHIPS, 2), side),
            *split((2,), side),
            *split((2, 2), side),
            vmem((conv_dev // COLORS + 1, cut, width_out)),
            vmem((stages - 1, conv_dev // COLORS, cut, width_out)),
            vmem((stages, engines, cut, width_out)),
            vmem((CUTS, COLORS * engines, cut, width_out)),
            dma(()),
            dma(()),
            dma((2 * CHIPS,)),
            dma((stages, engines)),
            dma((stages, engines)),
            dma((stages, CHIPS)),
            dma((stages, CHIPS)),
            dma((stages, 6)),
            dma((stages, 6)),
            dma((stages, engines)),
            dma((stages, engines)),
        ],
        compiler_params=pltpu.CompilerParams(
            collective_id=0, has_side_effects=True, vmem_limit_bytes=62 * 2**20
        ),
        cost_estimate=pl.CostEstimate(
            flops=2 * (tool_rows + conv_dev) * w_out.size, bytes_accessed=2 * (w_out.size + kv_pool.size), transcendentals=0
        ),
    )(
        new_slot.reshape(-1, 128), hist_len.reshape(-1, 128), page_table.T, kv_pool[:, 0], w_out,
        tool_q.reshape(conv_dev, CUTS, cut, width),
        tool_kv.reshape(conv_dev, CUTS, cut, 2 * head), dec_q, dec_kv[:, 0],
    )
    return dec_out, tool_out.reshape(tool_rows, width_out)


def solution(mesh):
    return jax.shard_map(
        local,
        mesh=mesh,
        in_specs=(
            P("engine", "tp", None, None),
            P("engine", None),
            P(),
            P(),
            P("engine", "tp"),
            P("engine", "tp", None),
            P("engine", "tp"),
            P("engine", "tp", None),
            P("tp", None),
        ),
        out_specs=(P("engine", "tp"), P("engine", "tp")),
        check_vma=False,
    )
```

```python
import functools
import math

import jax
import jax.numpy as jnp
from jax import lax
from jax.experimental import pallas as pl
from jax.experimental.pallas import tpu as pltpu
from jax.sharding import PartitionSpec as P

NEG = -1e30
MESH = pl.DeviceIdType.MESH
BF16, F32 = jnp.bfloat16, jnp.float32
MAXIMUM = 2**30
COLORS = 2
CUTS = 2
TOKENS_TOGETHER = 4
TOGETHER = 4
FINAL, CONV, DEST, HIST, HIST_NAT, BACK, PAGES, PAGES_NAT = 0, 1, 2, 3, 4, 5, 8, 16
CHIPS = 4


def plan(slot, hist, pages, me, engines, conv_dev, table):
    half = conv_dev // COLORS
    i32 = jnp.int32
    lane = lax.broadcasted_iota(i32, slot.shape, 1)
    local_id = lane % conv_dev
    engine = lax.broadcasted_iota(i32, slot.shape, 0) * (128 // conv_dev) + lane // conv_dev
    target, seat = slot // conv_dev, slot % conv_dev
    zero = jnp.zeros(slot.shape, i32)

    def earlier(v, d):
        return pltpu.roll(v, d, 1), local_id >= d

    def later(v, d):
        return pltpu.roll(v, 128 - d, 1), local_id < conv_dev - d

    rank, twins = zero, zero
    for d in range(1, conv_dev):
        v, ok = earlier(target, d)
        rank = rank + jnp.where(ok & (v == target), 1, 0)
        v, ok = later(target, d)
        twins = twins + jnp.where(ok & (v == target), 1, 0)
    doubled = jnp.where(rank + twins > 0, 1, 0)
    ahead, behind = zero, zero
    for d in range(1, conv_dev):
        v, ok = earlier(doubled, d)
        ahead = ahead + jnp.where(ok, v, 0)
        v, ok = later(doubled, d)
        behind = behind + jnp.where(ok, v, 0)
    pairs = (ahead + doubled + behind) // 2
    color = jnp.where(doubled > 0, rank, jnp.where(local_id - ahead >= half - pairs, 1, 0))
    place = zero
    for d in range(1, conv_dev):
        v, ok = earlier(color, d)
        place = place + jnp.where(ok & (v == color), 1, 0)
    rows = slot.shape[0]
    for c in range(COLORS):
        v = jnp.where((target == me) & (color == c), seat, 0)
        d = 1
        while d < conv_dev:
            v = v + pltpu.roll(v, 128 - d, 1)
            d *= 2
        table[16 + c * rows : 16 + (c + 1) * rows, :] = jnp.minimum(v, conv_dev - 1)
    sub = lax.broadcasted_iota(i32, (conv_dev, 128), 0)

    def gather(match, value):
        total = jnp.zeros((conv_dev, 128), i32)
        for r in range(rows):
            hit = jnp.broadcast_to(match[r : r + 1], sub.shape) == sub
            total = total + jnp.where(hit, jnp.broadcast_to(value[r : r + 1], sub.shape), 0)
        return jnp.sum(total, axis=1, keepdims=True)

    mine = engine == me
    row = jnp.where(mine, color * half + place, -1)
    conv = gather(row, local_id)
    columns = [
        gather(jnp.where(target == me, seat, -1), color * engines + engine),
        conv,
        gather(row, target),
        gather(row, hist),
        gather(jnp.where(mine, local_id, -1), hist),
    ] + [gather(jnp.where(mine & (color == c), target, -1), place) for c in range(COLORS)]
    wide = lax.broadcasted_iota(i32, (conv_dev, 128), 1)
    result = jnp.zeros((conv_dev, 128), i32)
    most = [COLORS * engines - 1, conv_dev - 1, engines - 1, MAXIMUM, MAXIMUM] + [half - 1] * COLORS
    for c, (v, top) in enumerate(zip(columns, most)):
        result = jnp.where(wide == c, jnp.clip(v, 0, top), result)
    for p in range(pages.shape[0]):
        line = jnp.broadcast_to(jnp.concatenate([pages[p : p + 1], jnp.zeros((1, 128 - conv_dev), i32)], axis=1), sub.shape)
        by_row = jnp.sum(jnp.where(wide == conv, line, 0), axis=1, keepdims=True)
        by_conv = jnp.sum(jnp.where(wide == sub, line, 0), axis=1, keepdims=True)
        result = jnp.where(wide == PAGES + p, by_row, jnp.where(wide == PAGES_NAT + p, by_conv, result))
    table[:16, :] = result


def attend(queries, pages, fresh, bias, near, scale):
    head = queries.shape[1]
    kv = jnp.concatenate(list(pages) + [fresh], axis=0)
    prefix = bias.shape[1]
    scores = lax.dot_general(queries, kv[:, :head], (((1,), (1,)), ((), ())), preferred_element_type=F32)
    near = jnp.concatenate([near] * (queries.shape[0] // near.shape[0]), axis=0)
    scores = jnp.concatenate([scores[:, :prefix] + bias, scores[:, prefix:] + near], axis=1)
    peak = jnp.max(scores, axis=1, keepdims=True)
    weights = jnp.exp2((scores - peak) * (scale * math.log2(math.e)))
    total = jnp.sum(weights, axis=1, keepdims=True)
    mixed = jnp.dot(weights.astype(BF16), kv[:, head:], preferred_element_type=F32)
    return mixed / total


def kernel(
    new_slot, hist_len, page_table, pool_hbm, w_hbm, tool_q, tool_kv, dec_q, dec_kv, out, dec_out,
    table, tab, kv16, pool, w, fsend, frecv_0, frecv_1, frecv_2, frecv_3, attn0, attn, heads, part0, part, got0, got, sums0, sums,
    two0, two, direct0, direct, rows0, rows, bsend, brecv,
    tab_sem, pool_sem, w_sem, fs, fr, xs, xr, ys, yr, bs, br,
    *, engines, conv_dev, pages_max,
):
    stages = COLORS * CUTS
    frecv = [frecv_0, frecv_1, frecv_2, frecv_3]
    half = conv_dev // COLORS
    cut = tool_q.shape[2]
    head = pool.shape[2] // 2
    width = tool_q.shape[3]
    group = width // head
    page = pool.shape[1]
    prefix = pages_max * page
    scale = head**-0.5
    width_out = w.shape[2]
    side = width_out // 2
    main = half * cut
    me, tp = lax.axis_index("engine"), lax.axis_index("tp")
    y, core = tp // 2, tp % 2
    partner = (me, y * 2 + 1 - core)
    up = (me, (y + 1) % CHIPS * 2 + core)
    down = (me, (y + CHIPS - 1) % CHIPS * 2 + core)
    other = lambda k: lax.rem(me + k, engines)

    barrier = pltpu.get_barrier_semaphore()

    @pl.loop(1, engines)
    def _(k):
        pl.semaphore_signal(barrier, inc=1, device_id=(other(k), tp), device_id_type=MESH)

    for peer in (partner, up, down):
        pl.semaphore_signal(barrier, inc=1, device_id=peer, device_id_type=MESH)

    load_pool = pltpu.make_async_copy(pool_hbm, pool, pool_sem)
    load_pool.start()

    def block_at(b):
        k = b // 2
        far = lax.rem(2 - k - k // 2 + 2 * (k // 3) + y + CHIPS, CHIPS)
        return far * 2 + lax.rem(core + 1 + b % 2, 2)

    def load_w(b):
        block = block_at(b)
        columns = pl.ds(pl.multiple_of(block * width_out, width_out), width_out)
        return pltpu.make_async_copy(w_hbm.at[:, columns], w.at[block], w_sem.at[block])

    @pl.loop(0, 2 * CHIPS)
    def _(b):
        load_w(b).start()

    plan(new_slot[...], hist_len[...], page_table[...], me, engines, conv_dev, table)
    load_tab = pltpu.make_async_copy(table, tab, tab_sem)
    load_tab.start()
    for h in range(group):
        heads[h] = dec_q[:, h * head : (h + 1) * head].astype(F32)
    dec_rows = dec_kv[...].astype(F32)
    for i in range(conv_dev):
        kv16[i] = jnp.broadcast_to(dec_rows[i : i + 1], (16, 2 * head)).astype(BF16)
    load_tab.wait()
    per_row = 128 // conv_dev

    def fill(ref, s, engine):
        slot = tab[16 + s // CUTS * (engines // per_row) + engine // per_row, engine % per_row * conv_dev]
        ref[engine, :, :width] = tool_q[slot, s % CUTS]
        ref[engine, :, width:] = tool_kv[slot, s % CUTS]

    def fwd(s, k):
        return pltpu.make_async_remote_copy(
            fsend.at[s, other(k)], frecv[s].at[me], fs.at[s, other(k)], fr.at[s, me],
            device_id=(other(k), tp), device_id_type=MESH,
        )

    def fwd_in(s, k):
        return pltpu.make_async_remote_copy(
            fsend.at[s, me], frecv[s].at[other(k)], fs.at[s, me], fr.at[s, other(k)],
            device_id=(other(k), tp), device_id_type=MESH,
        )

    def dispatch(s):
        @pl.loop(1, engines)
        def _(k):
            fill(fsend.at[s], s, other(k))

        if s == 0:
            pl.semaphore_wait(barrier, engines - 1 + 3)

        @pl.loop(1, engines)
        def _(k):
            fwd(s, k).start()

        fill(frecv[s], s, me)

    dispatch(0)
    dispatch(1)
    dispatch(2)
    dispatch(3)

    def pages_of(row, first):
        return [pool[tab[row, first + p]] for p in range(pages_max)]

    def bias_of(row, column):
        return jnp.where(lax.broadcasted_iota(jnp.int32, (1, prefix), 1) < tab[row, column], 0.0, NEG)

    col = lax.broadcasted_iota(jnp.int32, (16, page), 1)
    row = lax.broadcasted_iota(jnp.int32, (16, page), 0)

    load_pool.wait()
    only = jnp.where(col == 0, 0.0, NEG)

    def decode(step):
        at = [step * TOKENS_TOGETHER + n for n in range(TOKENS_TOGETHER)]
        results = []
        for i in at:
            fresh = jnp.concatenate([kv16[i], jnp.zeros((page - 16, 2 * head), BF16)], axis=0)
            q = jnp.concatenate(
                [heads[h, pl.ds(i, 1), :] for h in range(group)] + [jnp.zeros((16 - group, head), F32)], axis=0
            )
            results.append(attend(q.astype(BF16), pages_of(i, PAGES_NAT), fresh, bias_of(i, HIST_NAT), only, scale))
        for i, got_i in zip(at, results):
            for h in range(group):
                heads[h, pl.ds(i, 1), :] = got_i[h : h + 1]

    pl.loop(0, conv_dev // TOKENS_TOGETHER)(decode)

    for h in range(group):
        attn0[main:, h * head : (h + 1) * head] = heads[h].astype(BF16)

    def of(first, later, s):
        return first if s == 0 else later.at[s - 1]

    def attention(s, between):
        color, u = s // CUTS, s % CUTS

        @pl.loop(1, engines)
        def _(k):
            fwd_in(s, k).wait_recv()

        known = (u + 1) * cut
        near = jnp.where(((col <= row + u * cut) & (col < known)) | (col == known), 0.0, NEG)
        dst = of(attn0, attn, s)

        def one(j):
            at = color * half + j
            conv, dest = tab[at, CONV], tab[at, DEST]
            kv_new = [frecv[color * CUTS + v][dest, :, width:] for v in range(u + 1)]
            fresh = jnp.concatenate(
                kv_new + [kv16[conv], jnp.zeros((page - 16 - known, 2 * head), BF16)], axis=0
            )
            q = frecv[s][dest, :, :width]
            queries = jnp.concatenate([q[:, h * head : (h + 1) * head] for h in range(group)], axis=0)
            return attend(queries, pages_of(at, PAGES), fresh, bias_of(at, HIST), near, scale).astype(BF16)

        def some(first, count):
            @pl.loop(0, count // TOGETHER)
            def _(i):
                js = [first + i * TOGETHER + n for n in range(TOGETHER)]
                for j, got_j in [(j, one(j)) for j in js]:
                    for h in range(group):
                        dst[pl.ds(pl.multiple_of(j * cut, cut), cut), h * head : (h + 1) * head] = got_j[
                            h * cut : (h + 1) * cut
                        ]

        some(0, half // 2)
        between()
        some(half // 2, half // 2)

    def swap(s, k):
        return pltpu.make_async_remote_copy(
            of(part0, part, s).at[2 * k], of(got0, got, s).at[k], xs.at[s, k], xr.at[s, k],
            device_id=partner, device_id_type=MESH,
        )

    def hop(s, n, src, dst, to):
        return pltpu.make_async_remote_copy(src, dst, ys.at[s, n], yr.at[s, n], device_id=to, device_id_type=MESH)

    def ring(s):
        a, t, d = of(sums0, sums, s), of(two0, two, s), of(direct0, direct, s)
        return [
            hop(s, 0, a.at[0, 0], t.at[0], up),
            hop(s, 1, a.at[0, 1], t.at[1], down),
            hop(s, 2, a.at[1, 1], d.at[0, 1], up),
            hop(s, 3, a.at[2, 0], d.at[1, 0], down),
            hop(s, 4, a.at[1, 0], d.at[0, 0], up),
            hop(s, 5, a.at[2, 1], d.at[1, 1], down),
        ]

    def finish(s, k):
        swap(s, k).wait_recv()
        mine, came, a = of(part0, part, s), of(got0, got, s), of(sums0, sums, s)
        for v in range(2):
            cols = slice(v * side, (v + 1) * side)
            a[k, v] = mine[2 * k + 1, :, cols] + came[k, :, cols]

    def project(s):
        src, dst = of(attn0, attn, s), of(part0, part, s)
        steps = ring(s)

        @pl.loop(0, 2 * CHIPS)
        def _(b):
            k, block = b // 2, block_at(b)
            if s == 0:
                load_w(b).wait()
            dst[b] = jnp.dot(src[...], w[block], preferred_element_type=F32).astype(BF16)

            @pl.when(b % 2 == 0)
            def _():
                swap(s, k).start()

            @pl.when((b % 2 == 1) & (b > 1))
            def _():
                finish(s, k - 1)

            @pl.when(b == 3)
            def _():
                steps[0].start()
                steps[1].start()

            @pl.when(b == 5)
            def _():
                steps[2].start()

            @pl.when(b == 7)
            def _():
                steps[3].start()

        finish(s, CHIPS - 1)

    def relay(s):
        a, t, steps = of(sums0, sums, s), of(two0, two, s), ring(s)
        for v, k in ((0, 1), (1, 2)):
            steps[v].wait_recv()
            a[k, v] = a[k, v] + t[v]
            steps[4 + v].start()

    def back(s, k):
        color, u = s // CUTS, s % CUTS
        return pltpu.make_async_remote_copy(
            bsend.at[s, other(k)], brecv.at[u, color * engines + me], bs.at[s, other(k)], br.at[s, me],
            device_id=(other(k), tp), device_id_type=MESH,
        )

    def back_in(s, k):
        color, u = s // CUTS, s % CUTS
        return pltpu.make_async_remote_copy(
            bsend.at[s, me], brecv.at[u, color * engines + other(k)], bs.at[s, me], br.at[s, other(k)],
            device_id=(other(k), tp), device_id_type=MESH,
        )

    def deliver(s):
        color, u = s // CUTS, s % CUTS
        a, d, dst = of(sums0, sums, s), of(direct0, direct, s), of(rows0, rows, s)
        steps = ring(s)
        for n in range(2, 6):
            steps[n].wait_recv()
        for v in range(2):
            total = (a[3, v].astype(F32) + d[0, v].astype(F32) + d[1, v].astype(F32)).astype(BF16)
            dst[:, :, v * side : (v + 1) * side] = total.reshape(-1, cut, side)

        def mine(engine):
            place = tab[engine, BACK + color]
            return dst[place]

        @pl.loop(1, engines)
        def _(k):
            bsend[s, other(k)] = mine(other(k))
            back(s, k).start()

        brecv[u, color * engines + me] = mine(me)
        if s == 0:
            dec_out[...] = dst[half]

    for s in range(stages):
        attention(s, (lambda s=s: relay(s - 1)) if s > 0 else (lambda: None))
        project(s)
        if s > 0:
            deliver(s - 1)
    relay(stages - 1)
    deliver(stages - 1)

    for s in range(stages):

        @pl.loop(1, engines)
        def _(k, s=s):
            back_in(s, k).wait_recv()

    @pl.loop(0, conv_dev)
    def _(n):
        for u in range(CUTS):
            out[n, u] = brecv[u, tab[n, FINAL]]

    for s in range(stages):

        @pl.loop(1, engines)
        def _(k, s=s):
            fwd(s, k).wait_send()
            back(s, k).wait_send()

        for k in range(CHIPS):
            swap(s, k).wait_send()
        for step in ring(s):
            step.wait_send()


def local(kv_pool, page_table, hist_len, new_slot, dec_q, dec_kv, tool_q, tool_kv, w_out):
    engines = lax.axis_size("engine")
    conv_dev, pages_max = page_table.shape
    page, head = kv_pool.shape[2], kv_pool.shape[3] // 2
    width = dec_q.shape[1]
    group = width // head
    tool_rows = tool_q.shape[0]
    cut = tool_rows // conv_dev // CUTS
    width_out = w_out.shape[1] // (2 * CHIPS)
    side = width_out // 2
    stages = COLORS * CUTS
    main = conv_dev // COLORS * cut
    vmem = lambda shape: pltpu.VMEM(shape, BF16)
    split = lambda lead, cols: [
        vmem(lead + (main + conv_dev, cols)),
        vmem((stages - 1,) + lead + (main, cols)),
    ]
    dma = pltpu.SemaphoreType.DMA
    in_vmem = pl.BlockSpec(memory_space=pltpu.VMEM)
    anywhere = pl.BlockSpec(memory_space=pl.ANY)
    tool_out, dec_out = pl.pallas_call(
        functools.partial(kernel, engines=engines, conv_dev=conv_dev, pages_max=pages_max),
        out_shape=[
            jax.ShapeDtypeStruct((conv_dev, CUTS, cut, width_out), BF16),
            jax.ShapeDtypeStruct((conv_dev, width_out), BF16),
        ],
        in_specs=[in_vmem] * 3 + [anywhere] * 2 + [in_vmem] * 4,
        out_specs=[in_vmem, in_vmem],
        scratch_shapes=[
            pltpu.VMEM((24, 128), jnp.int32),
            pltpu.SMEM((24, 128), jnp.int32),
            vmem((conv_dev, 16, 2 * head)),
            vmem((kv_pool.shape[0], page, 2 * head)),
            vmem((2 * CHIPS, w_out.shape[0], width_out)),
            vmem((stages, engines, cut, width + 2 * head)),
            *[vmem((engines, cut, width + 2 * head)) for _ in range(stages)],
            *split((), width),
            pltpu.VMEM((group, conv_dev, head), F32),
            *split((2 * CHIPS,), width_out),
            *split((CHIPS,), width_out),
            *split((CHIPS, 2), side),
            *split((2,), side),
            *split((2, 2), side),
            vmem((conv_dev // COLORS + 1, cut, width_out)),
            vmem((stages - 1, conv_dev // COLORS, cut, width_out)),
            vmem((stages, engines, cut, width_out)),
            vmem((CUTS, COLORS * engines, cut, width_out)),
            dma(()),
            dma(()),
            dma((2 * CHIPS,)),
            dma((stages, engines)),
            dma((stages, engines)),
            dma((stages, CHIPS)),
            dma((stages, CHIPS)),
            dma((stages, 6)),
            dma((stages, 6)),
            dma((stages, engines)),
            dma((stages, engines)),
        ],
        compiler_params=pltpu.CompilerParams(
            collective_id=0, has_side_effects=True, vmem_limit_bytes=62 * 2**20
        ),
        cost_estimate=pl.CostEstimate(
            flops=2 * (tool_rows + conv_dev) * w_out.size, bytes_accessed=2 * (w_out.size + kv_pool.size), transcendentals=0
        ),
    )(
        new_slot.reshape(-1, 128), hist_len.reshape(-1, 128), page_table.T, kv_pool[:, 0], w_out,
        tool_q.reshape(conv_dev, CUTS, cut, width),
        tool_kv.reshape(conv_dev, CUTS, cut, 2 * head), dec_q, dec_kv[:, 0],
    )
    return dec_out, tool_out.reshape(tool_rows, width_out)


def solution(mesh):
    return jax.shard_map(
        local,
        mesh=mesh,
        in_specs=(
            P("engine", "tp", None, None),
            P("engine", None),
            P(),
            P(),
            P("engine", "tp"),
            P("engine", "tp", None),
            P("engine", "tp"),
            P("engine", "tp", None),
            P("tp", None),
        ),
        out_specs=(P("engine", "tp"), P("engine", "tp")),
        check_vma=False,
    )
```

```python
import functools
import math

import jax
import jax.numpy as jnp
from jax import lax
from jax.experimental import pallas as pl
from jax.experimental.pallas import tpu as pltpu
from jax.sharding import PartitionSpec as P

NEG = -1e30
MESH = pl.DeviceIdType.MESH
BF16, F32 = jnp.bfloat16, jnp.float32
MAXIMUM = 2**30
COLORS = 2
CUTS = 2
TOKENS_TOGETHER = 4
TOGETHER = 4
FINAL, CONV, DEST, HIST, HIST_NAT, BACK, PAGES, PAGES_NAT = 0, 1, 2, 3, 4, 5, 8, 16
CHIPS = 4


def plan(slot, hist, pages, me, engines, conv_dev, table):
    half = conv_dev // COLORS
    i32 = jnp.int32
    lane = lax.broadcasted_iota(i32, slot.shape, 1)
    local_id = lane % conv_dev
    engine = lax.broadcasted_iota(i32, slot.shape, 0) * (128 // conv_dev) + lane // conv_dev
    target, seat = slot // conv_dev, slot % conv_dev
    zero = jnp.zeros(slot.shape, i32)

    def earlier(v, d):
        return pltpu.roll(v, d, 1), local_id >= d

    def later(v, d):
        return pltpu.roll(v, 128 - d, 1), local_id < conv_dev - d

    rank, twins = zero, zero
    for d in range(1, conv_dev):
        v, ok = earlier(target, d)
        rank = rank + jnp.where(ok & (v == target), 1, 0)
        v, ok = later(target, d)
        twins = twins + jnp.where(ok & (v == target), 1, 0)
    doubled = jnp.where(rank + twins > 0, 1, 0)
    ahead, behind = zero, zero
    for d in range(1, conv_dev):
        v, ok = earlier(doubled, d)
        ahead = ahead + jnp.where(ok, v, 0)
        v, ok = later(doubled, d)
        behind = behind + jnp.where(ok, v, 0)
    pairs = (ahead + doubled + behind) // 2
    color = jnp.where(doubled > 0, rank, jnp.where(local_id - ahead >= half - pairs, 1, 0))
    place = zero
    for d in range(1, conv_dev):
        v, ok = earlier(color, d)
        place = place + jnp.where(ok & (v == color), 1, 0)
    rows = slot.shape[0]
    for c in range(COLORS):
        v = jnp.where((target == me) & (color == c), seat, 0)
        d = 1
        while d < conv_dev:
            v = v + pltpu.roll(v, 128 - d, 1)
            d *= 2
        table[16 + c * rows : 16 + (c + 1) * rows, :] = jnp.minimum(v, conv_dev - 1)
    sub = lax.broadcasted_iota(i32, (conv_dev, 128), 0)

    def gather(match, value):
        total = jnp.zeros((conv_dev, 128), i32)
        for r in range(rows):
            hit = jnp.broadcast_to(match[r : r + 1], sub.shape) == sub
            total = total + jnp.where(hit, jnp.broadcast_to(value[r : r + 1], sub.shape), 0)
        return jnp.sum(total, axis=1, keepdims=True)

    mine = engine == me
    row = jnp.where(mine, color * half + place, -1)
    conv = gather(row, local_id)
    columns = [
        gather(jnp.where(target == me, seat, -1), color * engines + engine),
        conv,
        gather(row, target),
        gather(row, hist),
        gather(jnp.where(mine, local_id, -1), hist),
    ] + [gather(jnp.where(mine & (color == c), target, -1), place) for c in range(COLORS)]
    wide = lax.broadcasted_iota(i32, (conv_dev, 128), 1)
    result = jnp.zeros((conv_dev, 128), i32)
    most = [COLORS * engines - 1, conv_dev - 1, engines - 1, MAXIMUM, MAXIMUM] + [half - 1] * COLORS
    for c, (v, top) in enumerate(zip(columns, most)):
        result = jnp.where(wide == c, jnp.clip(v, 0, top), result)
    for p in range(pages.shape[0]):
        line = jnp.broadcast_to(jnp.concatenate([pages[p : p + 1], jnp.zeros((1, 128 - conv_dev), i32)], axis=1), sub.shape)
        by_row = jnp.sum(jnp.where(wide == conv, line, 0), axis=1, keepdims=True)
        by_conv = jnp.sum(jnp.where(wide == sub, line, 0), axis=1, keepdims=True)
        result = jnp.where(wide == PAGES + p, by_row, jnp.where(wide == PAGES_NAT + p, by_conv, result))
    table[:16, :] = result


def attend(queries, pages, fresh, bias, near, scale):
    head = queries.shape[1]
    kv = jnp.concatenate(list(pages) + [fresh], axis=0)
    prefix = bias.shape[1]
    scores = lax.dot_general(queries, kv[:, :head], (((1,), (1,)), ((), ())), preferred_element_type=F32)
    near = jnp.concatenate([near] * (queries.shape[0] // near.shape[0]), axis=0)
    scores = jnp.concatenate([scores[:, :prefix] + bias, scores[:, prefix:] + near], axis=1)
    peak = jnp.max(scores, axis=1, keepdims=True)
    weights = jnp.exp2((scores - peak) * (scale * math.log2(math.e)))
    total = jnp.sum(weights, axis=1, keepdims=True)
    mixed = jnp.dot(weights.astype(BF16), kv[:, head:], preferred_element_type=F32)
    return mixed / total


def kernel(
    new_slot, hist_len, page_table, pool_hbm, w_hbm, tool_q, tool_kv, dec_q, dec_kv, out, dec_out,
    table, tab, kv16, pool, w, fsend, frecv_0, frecv_1, frecv_2, frecv_3, attn0, attn, heads, part0, part, got0, got, sums0, sums,
    two0, two, direct0, direct, rows0, rows, bsend, brecv,
    tab_sem, pool_sem, w_sem, fs, fr, xs, xr, ys, yr, bs, br,
    *, engines, conv_dev, pages_max,
):
    stages = COLORS * CUTS
    frecv = [frecv_0, frecv_1, frecv_2, frecv_3]
    half = conv_dev // COLORS
    cut = tool_q.shape[2]
    head = pool.shape[2] // 2
    width = tool_q.shape[3]
    group = width // head
    page = pool.shape[1]
    prefix = pages_max * page
    scale = head**-0.5
    width_out = w.shape[2]
    side = width_out // 2
    main = half * cut
    me, tp = lax.axis_index("engine"), lax.axis_index("tp")
    y, core = tp // 2, tp % 2
    partner = (me, y * 2 + 1 - core)
    up = (me, (y + 1) % CHIPS * 2 + core)
    down = (me, (y + CHIPS - 1) % CHIPS * 2 + core)
    other = lambda k: lax.rem(me + 7 * k, engines)

    barrier = pltpu.get_barrier_semaphore()

    @pl.loop(1, engines)
    def _(k):
        pl.semaphore_signal(barrier, inc=1, device_id=(other(k), tp), device_id_type=MESH)

    for peer in (partner, up, down):
        pl.semaphore_signal(barrier, inc=1, device_id=peer, device_id_type=MESH)

    load_pool = pltpu.make_async_copy(pool_hbm, pool, pool_sem)
    load_pool.start()

    def block_at(b):
        k = b // 2
        far = lax.rem(2 - k - k // 2 + 2 * (k // 3) + y + CHIPS, CHIPS)
        return far * 2 + lax.rem(core + 1 + b % 2, 2)

    def load_w(b):
        block = block_at(b)
        columns = pl.ds(pl.multiple_of(block * width_out, width_out), width_out)
        return pltpu.make_async_copy(w_hbm.at[:, columns], w.at[block], w_sem.at[block])

    @pl.loop(0, 2 * CHIPS)
    def _(b):
        load_w(b).start()

    plan(new_slot[...], hist_len[...], page_table[...], me, engines, conv_dev, table)
    load_tab = pltpu.make_async_copy(table, tab, tab_sem)
    load_tab.start()
    for h in range(group):
        heads[h] = dec_q[:, h * head : (h + 1) * head].astype(F32)
    dec_rows = dec_kv[...].astype(F32)
    for i in range(conv_dev):
        kv16[i] = jnp.broadcast_to(dec_rows[i : i + 1], (16, 2 * head)).astype(BF16)
    load_tab.wait()
    per_row = 128 // conv_dev

    def fill(ref, s, engine):
        slot = tab[16 + s // CUTS * (engines // per_row) + engine // per_row, engine % per_row * conv_dev]
        ref[engine, :, :width] = tool_q[slot, s % CUTS]
        ref[engine, :, width:] = tool_kv[slot, s % CUTS]

    def fwd(s, k):
        return pltpu.make_async_remote_copy(
            fsend.at[s, other(k)], frecv[s].at[me], fs.at[s, other(k)], fr.at[s, me],
            device_id=(other(k), tp), device_id_type=MESH,
        )

    def fwd_in(s, k):
        return pltpu.make_async_remote_copy(
            fsend.at[s, me], frecv[s].at[other(k)], fs.at[s, me], fr.at[s, other(k)],
            device_id=(other(k), tp), device_id_type=MESH,
        )

    def dispatch(s):
        @pl.loop(1, engines)
        def _(k):
            fill(fsend.at[s], s, other(k))

        if s == 0:
            pl.semaphore_wait(barrier, engines - 1 + 3)

        @pl.loop(1, engines)
        def _(k):
            fwd(s, k).start()

        fill(frecv[s], s, me)

    dispatch(0)
    dispatch(1)
    dispatch(2)
    dispatch(3)

    def pages_of(row, first):
        return [pool[tab[row, first + p]] for p in range(pages_max)]

    def bias_of(row, column):
        return jnp.where(lax.broadcasted_iota(jnp.int32, (1, prefix), 1) < tab[row, column], 0.0, NEG)

    col = lax.broadcasted_iota(jnp.int32, (16, page), 1)
    row = lax.broadcasted_iota(jnp.int32, (16, page), 0)

    load_pool.wait()
    only = jnp.where(col == 0, 0.0, NEG)

    def decode(step):
        at = [step * TOKENS_TOGETHER + n for n in range(TOKENS_TOGETHER)]
        results = []
        for i in at:
            fresh = jnp.concatenate([kv16[i], jnp.zeros((page - 16, 2 * head), BF16)], axis=0)
            q = jnp.concatenate(
                [heads[h, pl.ds(i, 1), :] for h in range(group)] + [jnp.zeros((16 - group, head), F32)], axis=0
            )
            results.append(attend(q.astype(BF16), pages_of(i, PAGES_NAT), fresh, bias_of(i, HIST_NAT), only, scale))
        for i, got_i in zip(at, results):
            for h in range(group):
                heads[h, pl.ds(i, 1), :] = got_i[h : h + 1]

    pl.loop(0, conv_dev // TOKENS_TOGETHER)(decode)

    for h in range(group):
        attn0[main:, h * head : (h + 1) * head] = heads[h].astype(BF16)

    def of(first, later, s):
        return first if s == 0 else later.at[s - 1]

    def attention(s, between):
        color, u = s // CUTS, s % CUTS

        @pl.loop(1, engines)
        def _(k):
            fwd_in(s, k).wait_recv()

        known = (u + 1) * cut
        near = jnp.where(((col <= row + u * cut) & (col < known)) | (col == known), 0.0, NEG)
        dst = of(attn0, attn, s)

        def one(j):
            at = color * half + j
            conv, dest = tab[at, CONV], tab[at, DEST]
            kv_new = [frecv[color * CUTS + v][dest, :, width:] for v in range(u + 1)]
            fresh = jnp.concatenate(
                kv_new + [kv16[conv], jnp.zeros((page - 16 - known, 2 * head), BF16)], axis=0
            )
            q = frecv[s][dest, :, :width]
            queries = jnp.concatenate([q[:, h * head : (h + 1) * head] for h in range(group)], axis=0)
            return attend(queries, pages_of(at, PAGES), fresh, bias_of(at, HIST), near, scale).astype(BF16)

        def some(first, count):
            @pl.loop(0, count // TOGETHER)
            def _(i):
                js = [first + i * TOGETHER + n for n in range(TOGETHER)]
                for j, got_j in [(j, one(j)) for j in js]:
                    for h in range(group):
                        dst[pl.ds(pl.multiple_of(j * cut, cut), cut), h * head : (h + 1) * head] = got_j[
                            h * cut : (h + 1) * cut
                        ]

        some(0, half // 2)
        between()
        some(half // 2, half // 2)

    def swap(s, k):
        return pltpu.make_async_remote_copy(
            of(part0, part, s).at[2 * k], of(got0, got, s).at[k], xs.at[s, k], xr.at[s, k],
            device_id=partner, device_id_type=MESH,
        )

    def hop(s, n, src, dst, to):
        return pltpu.make_async_remote_copy(src, dst, ys.at[s, n], yr.at[s, n], device_id=to, device_id_type=MESH)

    def ring(s):
        a, t, d = of(sums0, sums, s), of(two0, two, s), of(direct0, direct, s)
        return [
            hop(s, 0, a.at[0, 0], t.at[0], up),
            hop(s, 1, a.at[0, 1], t.at[1], down),
            hop(s, 2, a.at[1, 1], d.at[0, 1], up),
            hop(s, 3, a.at[2, 0], d.at[1, 0], down),
            hop(s, 4, a.at[1, 0], d.at[0, 0], up),
            hop(s, 5, a.at[2, 1], d.at[1, 1], down),
        ]

    def finish(s, k):
        swap(s, k).wait_recv()
        mine, came, a = of(part0, part, s), of(got0, got, s), of(sums0, sums, s)
        for v in range(2):
            cols = slice(v * side, (v + 1) * side)
            a[k, v] = mine[2 * k + 1, :, cols] + came[k, :, cols]

    def project(s):
        src, dst = of(attn0, attn, s), of(part0, part, s)
        steps = ring(s)

        @pl.loop(0, 2 * CHIPS)
        def _(b):
            k, block = b // 2, block_at(b)
            if s == 0:
                load_w(b).wait()
            dst[b] = jnp.dot(src[...], w[block], preferred_element_type=F32).astype(BF16)

            @pl.when(b % 2 == 0)
            def _():
                swap(s, k).start()

            @pl.when((b % 2 == 1) & (b > 1))
            def _():
                finish(s, k - 1)

            @pl.when(b == 3)
            def _():
                steps[0].start()
                steps[1].start()

            @pl.when(b == 5)
            def _():
                steps[2].start()

            @pl.when(b == 7)
            def _():
                steps[3].start()

        finish(s, CHIPS - 1)

    def relay(s):
        a, t, steps = of(sums0, sums, s), of(two0, two, s), ring(s)
        for v, k in ((0, 1), (1, 2)):
            steps[v].wait_recv()
            a[k, v] = a[k, v] + t[v]
            steps[4 + v].start()

    def back(s, k):
        color, u = s // CUTS, s % CUTS
        return pltpu.make_async_remote_copy(
            bsend.at[s, other(k)], brecv.at[u, color * engines + me], bs.at[s, other(k)], br.at[s, me],
            device_id=(other(k), tp), device_id_type=MESH,
        )

    def back_in(s, k):
        color, u = s // CUTS, s % CUTS
        return pltpu.make_async_remote_copy(
            bsend.at[s, me], brecv.at[u, color * engines + other(k)], bs.at[s, me], br.at[s, other(k)],
            device_id=(other(k), tp), device_id_type=MESH,
        )

    def deliver(s):
        color, u = s // CUTS, s % CUTS
        a, d, dst = of(sums0, sums, s), of(direct0, direct, s), of(rows0, rows, s)
        steps = ring(s)
        for n in range(2, 6):
            steps[n].wait_recv()
        for v in range(2):
            total = (a[3, v].astype(F32) + d[0, v].astype(F32) + d[1, v].astype(F32)).astype(BF16)
            dst[:, :, v * side : (v + 1) * side] = total.reshape(-1, cut, side)

        def mine(engine):
            place = tab[engine, BACK + color]
            return dst[place]

        @pl.loop(1, engines)
        def _(k):
            bsend[s, other(k)] = mine(other(k))
            back(s, k).start()

        brecv[u, color * engines + me] = mine(me)
        if s == 0:
            dec_out[...] = dst[half]

    for s in range(stages):
        attention(s, (lambda s=s: relay(s - 1)) if s > 0 else (lambda: None))
        project(s)
        if s > 0:
            deliver(s - 1)
    relay(stages - 1)
    deliver(stages - 1)

    for s in range(stages):

        @pl.loop(1, engines)
        def _(k, s=s):
            back_in(s, k).wait_recv()

    @pl.loop(0, conv_dev)
    def _(n):
        for u in range(CUTS):
            out[n, u] = brecv[u, tab[n, FINAL]]

    for s in range(stages):

        @pl.loop(1, engines)
        def _(k, s=s):
            fwd(s, k).wait_send()
            back(s, k).wait_send()

        for k in range(CHIPS):
            swap(s, k).wait_send()
        for step in ring(s):
            step.wait_send()


def local(kv_pool, page_table, hist_len, new_slot, dec_q, dec_kv, tool_q, tool_kv, w_out):
    engines = lax.axis_size("engine")
    conv_dev, pages_max = page_table.shape
    page, head = kv_pool.shape[2], kv_pool.shape[3] // 2
    width = dec_q.shape[1]
    group = width // head
    tool_rows = tool_q.shape[0]
    cut = tool_rows // conv_dev // CUTS
    width_out = w_out.shape[1] // (2 * CHIPS)
    side = width_out // 2
    stages = COLORS * CUTS
    main = conv_dev // COLORS * cut
    vmem = lambda shape: pltpu.VMEM(shape, BF16)
    split = lambda lead, cols: [
        vmem(lead + (main + conv_dev, cols)),
        vmem((stages - 1,) + lead + (main, cols)),
    ]
    dma = pltpu.SemaphoreType.DMA
    in_vmem = pl.BlockSpec(memory_space=pltpu.VMEM)
    anywhere = pl.BlockSpec(memory_space=pl.ANY)
    tool_out, dec_out = pl.pallas_call(
        functools.partial(kernel, engines=engines, conv_dev=conv_dev, pages_max=pages_max),
        out_shape=[
            jax.ShapeDtypeStruct((conv_dev, CUTS, cut, width_out), BF16),
            jax.ShapeDtypeStruct((conv_dev, width_out), BF16),
        ],
        in_specs=[in_vmem] * 3 + [anywhere] * 2 + [in_vmem] * 4,
        out_specs=[in_vmem, in_vmem],
        scratch_shapes=[
            pltpu.VMEM((24, 128), jnp.int32),
            pltpu.SMEM((24, 128), jnp.int32),
            vmem((conv_dev, 16, 2 * head)),
            vmem((kv_pool.shape[0], page, 2 * head)),
            vmem((2 * CHIPS, w_out.shape[0], width_out)),
            vmem((stages, engines, cut, width + 2 * head)),
            *[vmem((engines, cut, width + 2 * head)) for _ in range(stages)],
            *split((), width),
            pltpu.VMEM((group, conv_dev, head), F32),
            *split((2 * CHIPS,), width_out),
            *split((CHIPS,), width_out),
            *split((CHIPS, 2), side),
            *split((2,), side),
            *split((2, 2), side),
            vmem((conv_dev // COLORS + 1, cut, width_out)),
            vmem((stages - 1, conv_dev // COLORS, cut, width_out)),
            vmem((stages, engines, cut, width_out)),
            vmem((CUTS, COLORS * engines, cut, width_out)),
            dma(()),
            dma(()),
            dma((2 * CHIPS,)),
            dma((stages, engines)),
            dma((stages, engines)),
            dma((stages, CHIPS)),
            dma((stages, CHIPS)),
            dma((stages, 6)),
            dma((stages, 6)),
            dma((stages, engines)),
            dma((stages, engines)),
        ],
        compiler_params=pltpu.CompilerParams(
            collective_id=0, has_side_effects=True, vmem_limit_bytes=62 * 2**20
        ),
        cost_estimate=pl.CostEstimate(
            flops=2 * (tool_rows + conv_dev) * w_out.size, bytes_accessed=2 * (w_out.size + kv_pool.size), transcendentals=0
        ),
    )(
        new_slot.reshape(-1, 128), hist_len.reshape(-1, 128), page_table.T, kv_pool[:, 0], w_out,
        tool_q.reshape(conv_dev, CUTS, cut, width),
        tool_kv.reshape(conv_dev, CUTS, cut, 2 * head), dec_q, dec_kv[:, 0],
    )
    return dec_out, tool_out.reshape(tool_rows, width_out)


def solution(mesh):
    return jax.shard_map(
        local,
        mesh=mesh,
        in_specs=(
            P("engine", "tp", None, None),
            P("engine", None),
            P(),
            P(),
            P("engine", "tp"),
            P("engine", "tp", None),
            P("engine", "tp"),
            P("engine", "tp", None),
            P("tp", None),
        ),
        out_specs=(P("engine", "tp"), P("engine", "tp")),
        check_vma=False,
    )
```
